128 devices in a mesh: leaf: 8 (over z, core), space: 16 (over y, x).
Axes of the slice: x: 4, y: 4, z: 4, core: 2. Of those that a mesh axis runs over, the one named last changes fastest.
Arguments:
- fine_density: bfloat16 [152, 524288], P(None, ('leaf', 'space')), may hold values from -6 to 6
- m2m_ops: bfloat16 [8, 152, 152], replicated, may hold values from -0.3125 to 0.3125
- m2l_ops: bfloat16 [316, 152, 152], replicated, may hold values from -0.078125 to 0.078125
- parent_slot: int32 [524288], P(('leaf', 'space')), may hold values from 0 to 8191, as said below
- octant: int32 [524288], P(('leaf', 'space')), may hold values from 0 to 7
- send_rows: int32 [2048, 1024], P(('leaf', 'space')), may hold values from 0 to 4095, as said below
- batch_op: int32 [65536], P(('leaf', 'space')), may hold values from 0 to 315
- batch_source_entry: int32 [65536, 256], P(('leaf', 'space')), may hold values from 0 to 20479, as said below
- batch_tgt: int32 [65536, 256], P(('leaf', 'space')), may hold values from 0 to 4096, as said below
Outputs:
- local_coeffs: float32 [152, 524288], P(None, ('leaf', 'space'))
- coarse_density: float32 [152, 16, 8192], P(None, 'space', 'leaf')
The draws below stay inside these ranges and needn't reach their ends.
Inputs may be any that keep to these rules, and one draw needn't show every extreme that they name: parent_slot // 1024 is the leaf index of the parent's owner; boxes with the same parent have different octants. `send_rows`: row q of device (l, s) lists 1024 distinct local boxes of (l, s) that device (l, q) reads. `batch_source_entry`: below 4096: a box of the device itself; 4096 + p * 1024 + k: slot k of what device (l, p) provides, p never the device's own space index; a dead slot holds 0. `batch_tgt`: in every batch the live slots come first; their number is the same for all batches of one device, at least 16, and 256 on at least one device; 4096 marks a dead slot.
All inputs are finite; a program needn't handle non-finite values.
Results may differ from the reference program's by a relative error of at most 0.0003.
Values may be sent and summed in bfloat16 or wider, within the bound.
A program may use at most 256 MiB of HBM per device.

```python
import math
import jax
import jax.numpy as jnp
from jax import lax

P_SIZE = 152
NOPS = 316
LIST = 32
BS = 256
BOX_DEV = 4096
CAP = 1024
NPC = 8192
NB = 512
NBOX = 524288
N_LEAF = 8
N_SPACE = 16
DEVICES = 128


def tree_slots(key):
    key = jax.random.fold_in(key, 101)
    keys = jax.random.split(key, N_SPACE)
    perms = jax.vmap(lambda single: jax.random.permutation(single, 8 * NPC)[:BOX_DEV * N_LEAF])(keys)
    return perms.reshape(N_SPACE, N_LEAF, BOX_DEV).transpose(1, 0, 2).reshape(-1).astype(jnp.int32)


def slot_tables(key):
    key = jax.random.fold_in(key, 202)
    keys = jax.random.split(key, 7)
    rows = DEVICES * NB
    live_count = jax.random.randint(keys[0], (DEVICES,), max(BS // 16, 1), BS + 1)
    full_device = jax.random.randint(keys[1], (), 0, DEVICES)
    live_count = jnp.where(jnp.arange(DEVICES) == full_device, BS, live_count)
    device = jnp.arange(rows) // NB
    live = jnp.arange(BS)[None, :] < live_count[device][:, None]
    space_index = device % N_SPACE
    local = jax.random.randint(keys[2], (rows, BS), 0, 4) == 0
    own_box = jax.random.randint(keys[3], (rows, BS), 0, BOX_DEV)
    offset = jax.random.randint(keys[4], (rows, BS), 1, N_SPACE)
    peer = (space_index[:, None] + offset) % N_SPACE
    batch_slot_index = jax.random.randint(keys[5], (rows, BS), 0, CAP)
    remote = BOX_DEV + peer * CAP + batch_slot_index
    source = jnp.where(live, jnp.where(local, own_box, remote), 0)
    target = jnp.where(live, jax.random.randint(keys[6], (rows, BS), 0, BOX_DEV), BOX_DEV)
    return (source.astype(jnp.int32), target.astype(jnp.int32))


def draw_parent_slot(key, part):
    slots = tree_slots(key)
    return slots // 8


def draw_octant(key, part):
    slots = tree_slots(key)
    return slots % 8


def draw_send_rows(key, part):
    key = jax.random.fold_in(key, 3)
    keys = jax.random.split(key, DEVICES * N_SPACE)
    rows = jax.vmap(lambda single: jax.random.permutation(single, BOX_DEV)[:CAP])(keys)
    return rows.astype(jnp.int32)


def draw_batch_source_entry(key, part):
    source, target = slot_tables(key)
    return source


def draw_batch_tgt(key, part):
    source, target = slot_tables(key)
    return target


def with_ends(result, rng, low, high):
    extent = result.shape
    spot = [jax.random.randint(jax.random.fold_in(rng, axis), (), 0, extent[axis]) for axis in range(len(extent))]
    result = result.at[tuple(spot)].set(low)
    longest = extent.index(max(extent))
    spot[longest] = (spot[longest] + 1) % extent[longest]
    return result.at[tuple(spot)].set(high)


def shard_levels(stream_key, extent, pieces, least, high):
    def one(dim, blocks):
        steps = jax.random.uniform(jax.random.fold_in(jax.random.fold_in(stream_key, 6), dim), (blocks,), jnp.float32, least / len(pieces), high / len(pieces))
        return jnp.repeat(jnp.exp(steps), extent[dim] // blocks).reshape((-1,) + (1,) * (len(extent) - dim - 1))

    factor_of = one(*pieces[0])
    for cut in pieces[1:]:
        factor_of = factor_of * one(*cut)
    return factor_of


def bell_draw(rng, shape, spread, reach, cuts=(), kind=jnp.bfloat16):
    factor_of = shard_levels(rng, shape, cuts, -0.22, 0.18) if cuts else 1.0
    values = jax.random.normal(rng, shape, jnp.float32) * spread * factor_of
    return jnp.minimum(jnp.maximum(values, -reach), reach).astype(kind)


def setup_inputs(seed: int = 0) -> dict:
    splits = jax.random.split(jax.random.key(seed), 10)
    return {
        "fine_density": bell_draw(splits[0], (P_SIZE, NBOX), 1.0, 6.0, ((1, 128),)),
        "m2m_ops": bell_draw(splits[1], (8, P_SIZE, P_SIZE), (2 * P_SIZE) ** -0.5, 0.3125),
        "m2l_ops": bell_draw(splits[2], (NOPS, P_SIZE, P_SIZE), (P_SIZE * LIST) ** -0.5, 0.078125),
        "parent_slot": draw_parent_slot(jax.random.fold_in(splits[9], 71), 0),
        "octant": draw_octant(jax.random.fold_in(splits[9], 71), 0),
        "send_rows": draw_send_rows(jax.random.fold_in(splits[9], 71), 0),
        "batch_op": with_ends(jax.random.randint(splits[6], (DEVICES * NB,), 0, NOPS), jax.random.fold_in(splits[6], 1), 0, NOPS - 1).astype(jnp.int32),
        "batch_source_entry": draw_batch_source_entry(jax.random.fold_in(splits[9], 71), 0),
        "batch_tgt": draw_batch_tgt(jax.random.fold_in(splits[9], 71), 0),
    }


def upward_merge(fine_density, m2m_ops, parent_slot, octant):
    translated = jnp.zeros((P_SIZE, NBOX), jnp.float32)
    for octant_id in range(8):
        shifted = jnp.dot(m2m_ops[octant_id], fine_density, preferred_element_type=jnp.float32)
        translated = translated + jnp.where(octant[None, :] == octant_id, shifted, jnp.float32(0.0))
    column_index = (jnp.arange(NBOX, dtype=jnp.int32) // BOX_DEV) % N_SPACE
    flat_index = column_index * NPC + parent_slot
    merged = jnp.zeros((P_SIZE, N_SPACE * NPC), jnp.float32).at[:, flat_index].add(translated)
    return merged.reshape(P_SIZE, N_SPACE, NPC)


def translate_lists(fine_density, m2l_ops, send_rows, batch_op, batch_source_entry, batch_tgt):
    grouping = math.gcd(NB, 64)
    block_count = DEVICES * NB // grouping
    sources_all = fine_density.astype(jnp.float32)
    operators_all = m2l_ops.astype(jnp.float32)
    device_owner_map = jnp.arange(block_count, dtype=jnp.int32) // (NB // grouping)
    scanned = (batch_op.reshape(block_count, grouping), batch_source_entry.reshape(block_count, grouping, BS),
               batch_tgt.reshape(block_count, grouping, BS), device_owner_map)

    def visit(totals, entry):
        op_index, src_index, tgt_index, device = entry
        leaf_index = device // N_SPACE
        space_index = device % N_SPACE
        remote_portion = jnp.maximum(src_index - BOX_DEV, 0)
        peer_space = remote_portion // CAP
        batch_slot_index = remote_portion % CAP
        peer_device = leaf_index * N_SPACE + peer_space
        remote_box = send_rows[peer_device * N_SPACE + space_index, batch_slot_index]
        global_source = jnp.where(src_index < BOX_DEV, device * BOX_DEV + src_index,
                                  peer_device * BOX_DEV + remote_box).astype(jnp.int32)
        gathered_rows = jnp.take(sources_all, global_source, axis=1)
        translation_operators = operators_all[op_index]
        product = jnp.einsum("gqp,pgb->qgb", translation_operators, gathered_rows, precision=lax.Precision.HIGHEST)
        global_target_box = jnp.where(tgt_index < BOX_DEV, device * BOX_DEV + tgt_index, NBOX).astype(jnp.int32)
        totals = totals.at[:, global_target_box.reshape(-1)].add(product.reshape(P_SIZE, -1), mode="drop")
        return totals, None

    totals, _ = lax.scan(visit, jnp.zeros((P_SIZE, NBOX), jnp.float32), scanned)
    return totals


def reference(fine_density, m2m_ops, m2l_ops, parent_slot, octant, send_rows, batch_op, batch_source_entry, batch_tgt):
    coarse_density = upward_merge(fine_density, m2m_ops, parent_slot, octant)
    local_coeffs = translate_lists(fine_density, m2l_ops, send_rows, batch_op, batch_source_entry, batch_tgt)
    return local_coeffs, coarse_density
```

```python
import functools

import jax
import jax.numpy as jnp
from jax import lax
from jax.experimental import pallas as pl
from jax.experimental.pallas import tpu as pltpu
from jax.sharding import PartitionSpec as P

LANES = 128
CHUNK = 256
GROUP = 4
COPIES = 4
PARTS = 4
VMEM_LIMIT = 62 * 2**20


def rows_to_pairs(values, ref, first, count):
    points = values.shape[1]
    tail = jnp.concatenate(
        [values[:, LANES:], jnp.zeros((count, 2 * LANES - points), values.dtype)], axis=1
    )
    ref[pl.ds(2 * first, count, stride=2), :] = values[:, :LANES]
    ref[pl.ds(2 * first + 1, count, stride=2), :] = tail


def columns_to_pairs(columns_ref, ref):
    points, count = columns_ref.shape

    def body(step, carry):
        first = pl.multiple_of(step * CHUNK, CHUNK)
        columns = columns_ref[:, pl.ds(first, CHUNK)].astype(jnp.float32)
        rows_to_pairs(columns.T, ref, first, CHUNK)
        return carry

    lax.fori_loop(0, count // CHUNK, body, 0)


def pairs_to_columns(refs, out_ref):
    points, count = out_ref.shape

    def body(step, carry):
        first = pl.multiple_of(step * CHUNK, CHUNK)
        head = refs[0][pl.ds(2 * first, CHUNK, stride=2), :]
        tail = refs[0][pl.ds(2 * first + 1, CHUNK, stride=2), :]
        for ref in refs[1:]:
            head = head + ref[pl.ds(2 * first, CHUNK, stride=2), :]
            tail = tail + ref[pl.ds(2 * first + 1, CHUNK, stride=2), :]
        out_ref[pl.ds(0, LANES), pl.ds(first, CHUNK)] = head.T
        out_ref[pl.ds(LANES, points - LANES), pl.ds(first, CHUNK)] = tail.T[: points - LANES]
        return carry

    lax.fori_loop(0, count // CHUNK, body, 0)


def clear(refs):
    def body(step, carry):
        for ref in refs:
            ref[pl.ds(pl.multiple_of(step * 16, 16), 16), :] = jnp.zeros((16, LANES), ref.dtype)
        return carry

    lax.fori_loop(0, refs[0].shape[0] // 16, body, 0)


def pack_kernel(rows_ref, fine_ref, out_ref, table, staged):
    @pl.when(pl.program_id(0) == 0)
    def _():
        columns_to_pairs(fine_ref, table)

    capacity = rows_ref.shape[2]
    unroll = 128

    def gather(step, carry):
        base = step * unroll
        for k in range(unroll):
            row = pl.multiple_of(rows_ref[0, 0, base + k], 2)
            staged[pl.ds(pl.multiple_of(2 * base, 2 * unroll) + 2 * k, 2), :] = table[pl.ds(row, 2), :]
        return carry

    lax.fori_loop(0, capacity // unroll, gather, 0)
    quarter = capacity // PARTS
    tails = staged[pl.ds(1, quarter, stride=2), :]
    for part in range(PARTS):
        start = 2 * part * quarter
        out_ref[0, pl.ds(part * quarter, quarter), :] = staged[
            pl.ds(start, quarter, stride=2), :
        ].astype(jnp.bfloat16)
        if part:
            tail = staged[pl.ds(start + 1, quarter, stride=2), :]
            tails = tails + pltpu.roll(tail, part * (LANES // PARTS), 1)
    out_ref[0, pl.ds(capacity, quarter), :] = tails.astype(jnp.bfloat16)


def pack_blocks(fine_density, send_rows):
    points, box_count = fine_density.shape
    peers, capacity = send_rows.shape
    packed = capacity + capacity // PARTS
    return pl.pallas_call(
        pack_kernel,
        grid=(peers,),
        in_specs=[
            pl.BlockSpec((1, 1, capacity), lambda q: (q, 0, 0), memory_space=pltpu.SMEM),
            pl.BlockSpec(memory_space=pltpu.VMEM),
        ],
        out_specs=pl.BlockSpec((1, packed, LANES), lambda q: (q, 0, 0)),
        out_shape=jax.ShapeDtypeStruct((peers, packed, LANES), jnp.bfloat16),
        scratch_shapes=[
            pltpu.VMEM((2 * box_count, LANES), jnp.float32),
            pltpu.VMEM((2 * capacity, LANES), jnp.float32),
        ],
        compiler_params=pltpu.CompilerParams(vmem_limit_bytes=VMEM_LIMIT),
        name="pack_blocks",
    )((2 * send_rows)[:, None, :], fine_density)


def merge_kernel(slot_ref, octant_ref, fine_ref, m2m_ref, out_ref, moved, *sums):
    points, box_count = fine_ref.shape
    clear(sums)

    def translate(step, carry):
        first = pl.multiple_of(step * CHUNK, CHUNK)
        columns = fine_ref[:, pl.ds(first, CHUNK)]
        octants = octant_ref[:, pl.ds(first, CHUNK)]
        total = jnp.zeros((points, CHUNK), jnp.float32)
        for octant in range(8):
            shifted = jnp.dot(m2m_ref[octant], columns, preferred_element_type=jnp.float32)
            total = total + jnp.where(octants == octant, shifted, jnp.float32(0.0))
        rows_to_pairs(total.T, moved, first, CHUNK)
        return carry

    lax.fori_loop(0, box_count // CHUNK, translate, 0)
    unroll = 64

    def scatter(step, carry):
        base = step * unroll
        first = pl.multiple_of(2 * base, 2 * unroll)
        for k in range(0, unroll, COPIES):
            at = [pl.multiple_of(slot_ref[0, base + k + c], 2) for c in range(COPIES)]
            new = [
                sums[c][pl.ds(at[c], 2), :] + moved[pl.ds(first + 2 * (k + c), 2), :]
                for c in range(COPIES)
            ]
            for c in range(COPIES):
                sums[c][pl.ds(at[c], 2), :] = new[c]
        return carry

    lax.fori_loop(0, box_count // unroll, scatter, 0)
    pairs_to_columns(sums, out_ref)


def merge_upward(fine_density, m2m_ops, parent_slot, octant, parent_count):
    points, box_count = fine_density.shape
    vmem = pl.BlockSpec(memory_space=pltpu.VMEM)
    return pl.pallas_call(
        merge_kernel,
        in_specs=[pl.BlockSpec(memory_space=pltpu.SMEM), vmem, vmem, vmem],
        out_specs=vmem,
        out_shape=jax.ShapeDtypeStruct((points, parent_count), jnp.float32),
        scratch_shapes=[pltpu.VMEM((2 * box_count, LANES), jnp.float32)]
        + [pltpu.VMEM((2 * parent_count, LANES), jnp.float32)] * COPIES,
        compiler_params=pltpu.CompilerParams(vmem_limit_bytes=VMEM_LIMIT),
        name="merge_upward",
    )((2 * parent_slot)[None, :], octant[None, :], fine_density, m2m_ops)


def translate_kernel(slots, op_ref, index_hbm, fine_ref, blocks_ref, *refs):
    ops, refs = refs[:GROUP], refs[GROUP:]
    out_ref, refs = refs[0], refs[1:]
    table, refs = refs[0], refs[1:]
    gathered, refs = refs[:2], refs[2:]
    products, refs = refs[:2], refs[2:]
    index, refs = refs[:GROUP], refs[GROUP:]
    sem, totals = refs[0], refs[1:]
    step, steps = pl.program_id(0), pl.num_programs(0)
    points, box_count = fine_ref.shape

    def index_copy(which, batch):
        return pltpu.make_async_copy(index_hbm.at[batch], index[which], sem.at[which])

    @pl.when(step == 0)
    def _():
        for which in range(GROUP):
            index_copy(which, which).start()
        clear(gathered)
        clear(products)
        clear(totals)
        columns_to_pairs(fine_ref, table)
        peers, packed, _ = blocks_ref.shape
        capacity = packed // (PARTS + 1) * PARTS
        quarter = capacity // PARTS
        lane = lax.broadcasted_iota(jnp.int32, (quarter, LANES), 1)

        def unpack(peer, carry):
            tails = blocks_ref[peer, pl.ds(capacity, quarter), :].astype(jnp.float32)
            for part in range(PARTS):
                first = pl.multiple_of(2 * (box_count + peer * capacity), 2 * quarter)
                first = first + 2 * part * quarter
                head = blocks_ref[peer, pl.ds(part * quarter, quarter), :]
                tail = pltpu.roll(tails, (PARTS - part) % PARTS * (LANES // PARTS), 1) if part else tails
                tail = jnp.where(lane < points - LANES, tail, jnp.float32(0.0))
                table[pl.ds(first, quarter, stride=2), :] = head.astype(jnp.float32)
                table[pl.ds(first + 1, quarter, stride=2), :] = tail
            return carry

        lax.fori_loop(0, peers, unpack, 0)

    for which in range(GROUP):
        now, before = which % 2, 1 - which % 2
        index_copy(which, step * GROUP + which).wait()
        columns = jnp.concatenate(
            [
                gathered[before][pl.ds(0, slots, stride=2), :],
                gathered[before][pl.ds(1, slots, stride=2), :],
            ],
            axis=1,
        )[:, :points].astype(jnp.bfloat16)
        product = lax.dot_general(
            columns, ops[which][0], (((1,), (1,)), ((), ())), preferred_element_type=jnp.float32
        )
        products[before][pl.ds(0, slots, stride=2), :] = product[:, :LANES]
        products[before][pl.ds(1, slots, stride=2), pl.ds(0, points - LANES)] = product[:, LANES:]
        for k in range(0, slots, COPIES):
            at = [pl.multiple_of(index[which][0, slots + k + c], 2) for c in range(COPIES)]
            new = [
                totals[c][pl.ds(at[c], 2), :] + products[now][pl.ds(2 * (k + c), 2), :]
                for c in range(COPIES)
            ]
            for c in range(COPIES):
                totals[c][pl.ds(at[c], 2), :] = new[c]
            for c in range(COPIES):
                row = pl.multiple_of(index[which][0, k + c], 2)
                gathered[now][pl.ds(2 * (k + c), 2), :] = table[pl.ds(row, 2), :]
        index_copy(which, (step + 1) * GROUP + which).start()

    @pl.when(step == steps - 1)
    def _():
        for which in range(GROUP):
            index_copy(which, (step + 1) * GROUP + which).wait()
        pairs_to_columns(totals, out_ref)


def translate_lists(fine_density, blocks, m2l_ops, batch_op, source_entry, target):
    points, box_count = fine_density.shape
    batches, slots = source_entry.shape
    peers, packed, _ = blocks.shape
    capacity = packed // (PARTS + 1) * PARTS
    steps = -(-(batches + 2) // GROUP)
    padded = (steps + 1) * GROUP
    source = jnp.pad(2 * source_entry, ((0, padded - batches), (0, 0)))
    target = jnp.pad(
        2 * target, ((2, padded - batches - 2), (0, 0)), constant_values=2 * box_count
    )
    index = jnp.concatenate([source, target], axis=1)[:, None, :]
    op_index = jnp.pad(batch_op, (1, padded - batches - 1))
    vmem = pl.BlockSpec(memory_space=pltpu.VMEM)
    operators = [
        pl.BlockSpec((1, points, points), lambda j, ops, which=which: (ops[j * GROUP + which], 0, 0))
        for which in range(GROUP)
    ]
    return pl.pallas_call(
        functools.partial(translate_kernel, slots),
        grid_spec=pltpu.PrefetchScalarGridSpec(
            num_scalar_prefetch=1,
            grid=(steps,),
            in_specs=[pl.BlockSpec(memory_space=pl.ANY), vmem, vmem] + operators,
            out_specs=vmem,
            scratch_shapes=[pltpu.VMEM((2 * (box_count + peers * capacity), LANES), jnp.float32)]
            + [pltpu.VMEM((2 * slots, LANES), jnp.float32)] * 4
            + [pltpu.SMEM((1, 2 * slots), jnp.int32)] * GROUP
            + [pltpu.SemaphoreType.DMA((GROUP,))]
            + [pltpu.VMEM((2 * (box_count + 8), LANES), jnp.float32)] * COPIES,
        ),
        out_shape=jax.ShapeDtypeStruct((points, box_count), jnp.float32),
        compiler_params=pltpu.CompilerParams(
            vmem_limit_bytes=VMEM_LIMIT, dimension_semantics=("arbitrary",)
        ),
        name="translate_lists",
    )(op_index, index, fine_density, blocks, *[m2l_ops] * GROUP)


def per_device(
    fine_density,
    m2m_ops,
    m2l_ops,
    parent_slot,
    octant,
    send_rows,
    batch_op,
    batch_source_entry,
    batch_tgt,
):
    points, box_count = fine_density.shape
    parent_count = box_count // 4 * lax.axis_size("leaf")
    blocks = pack_blocks(fine_density, send_rows)
    blocks = lax.all_to_all(blocks, "space", 0, 0, tiled=True)
    partial_sums = merge_upward(fine_density, m2m_ops, parent_slot, octant, parent_count)
    coarse_level = lax.psum_scatter(partial_sums, "leaf", scatter_dimension=1, tiled=True)
    local_coeffs = translate_lists(
        fine_density, blocks, m2l_ops, batch_op, batch_source_entry, batch_tgt
    )
    return (local_coeffs, coarse_level[:, None, :])


def solution(mesh):
    return jax.shard_map(
        per_device,
        mesh=mesh,
        in_specs=(
            P(None, ("leaf", "space")),
            P(),
            P(),
            P(("leaf", "space")),
            P(("leaf", "space")),
            P(("leaf", "space"), None),
            P(("leaf", "space")),
            P(("leaf", "space"), None),
            P(("leaf", "space"), None),
        ),
        out_specs=(P(None, ("leaf", "space")), P(None, "space", "leaf")),
        check_vma=False,
    )
```

```python
import functools

import jax
import jax.numpy as jnp
from jax import lax
from jax.experimental import pallas as pl
from jax.experimental.pallas import tpu as pltpu
from jax.sharding import PartitionSpec as P

LANES = 128
CHUNK = 256
GROUP = 4
SPAN = 1
COPIES = 8
MERGE_COPIES = 4
PARTS = 4
VMEM_LIMIT = 62 * 2**20


def rows_to_pairs(values, ref, first, count):
    points = values.shape[1]
    tail = jnp.concatenate(
        [values[:, LANES:], jnp.zeros((count, 2 * LANES - points), values.dtype)], axis=1
    )
    ref[pl.ds(2 * first, count, stride=2), :] = values[:, :LANES]
    ref[pl.ds(2 * first + 1, count, stride=2), :] = tail


def columns_to_pairs(columns_ref, ref):
    points, count = columns_ref.shape

    def body(step, carry):
        first = pl.multiple_of(step * CHUNK, CHUNK)
        columns = columns_ref[:, pl.ds(first, CHUNK)].astype(jnp.float32)
        rows_to_pairs(columns.T, ref, first, CHUNK)
        return carry

    lax.fori_loop(0, count // CHUNK, body, 0)


def pairs_to_columns(refs, out_ref):
    points, count = out_ref.shape

    def body(step, carry):
        first = pl.multiple_of(step * CHUNK, CHUNK)
        head = refs[0][pl.ds(2 * first, CHUNK, stride=2), :]
        tail = refs[0][pl.ds(2 * first + 1, CHUNK, stride=2), :]
        for ref in refs[1:]:
            head = head + ref[pl.ds(2 * first, CHUNK, stride=2), :]
            tail = tail + ref[pl.ds(2 * first + 1, CHUNK, stride=2), :]
        out_ref[pl.ds(0, LANES), pl.ds(first, CHUNK)] = head.T
        out_ref[pl.ds(LANES, points - LANES), pl.ds(first, CHUNK)] = tail.T[: points - LANES]
        return carry

    lax.fori_loop(0, count // CHUNK, body, 0)


def clear(refs):
    def body(step, carry):
        for ref in refs:
            ref[pl.ds(pl.multiple_of(step * 16, 16), 16), :] = jnp.zeros((16, LANES), ref.dtype)
        return carry

    lax.fori_loop(0, refs[0].shape[0] // 16, body, 0)


def pack_kernel(rows_ref, fine_ref, out_ref, table, staged):
    @pl.when(pl.program_id(0) == 0)
    def _():
        columns_to_pairs(fine_ref, table)

    capacity = rows_ref.shape[2]
    unroll = 128

    def gather(step, carry):
        base = step * unroll
        for k in range(unroll):
            row = pl.multiple_of(rows_ref[0, 0, base + k], 2)
            staged[pl.ds(pl.multiple_of(2 * base, 2 * unroll) + 2 * k, 2), :] = table[pl.ds(row, 2), :]
        return carry

    lax.fori_loop(0, capacity // unroll, gather, 0)
    quarter = capacity // PARTS
    tails = staged[pl.ds(1, quarter, stride=2), :]
    for part in range(PARTS):
        start = 2 * part * quarter
        out_ref[0, pl.ds(part * quarter, quarter), :] = staged[
            pl.ds(start, quarter, stride=2), :
        ].astype(jnp.bfloat16)
        if part:
            tail = staged[pl.ds(start + 1, quarter, stride=2), :]
            tails = tails + pltpu.roll(tail, part * (LANES // PARTS), 1)
    out_ref[0, pl.ds(capacity, quarter), :] = tails.astype(jnp.bfloat16)


def pack_blocks(fine_density, send_rows):
    points, box_count = fine_density.shape
    peers, capacity = send_rows.shape
    packed = capacity + capacity // PARTS
    return pl.pallas_call(
        pack_kernel,
        grid=(peers,),
        in_specs=[
            pl.BlockSpec((1, 1, capacity), lambda q: (q, 0, 0), memory_space=pltpu.SMEM),
            pl.BlockSpec(memory_space=pltpu.VMEM),
        ],
        out_specs=pl.BlockSpec((1, packed, LANES), lambda q: (q, 0, 0)),
        out_shape=jax.ShapeDtypeStruct((peers, packed, LANES), jnp.bfloat16),
        scratch_shapes=[
            pltpu.VMEM((2 * box_count, LANES), jnp.float32),
            pltpu.VMEM((2 * capacity, LANES), jnp.float32),
        ],
        compiler_params=pltpu.CompilerParams(vmem_limit_bytes=VMEM_LIMIT),
        name="pack_blocks",
    )((2 * send_rows)[:, None, :], fine_density)


def merge_kernel(slot_ref, octant_ref, fine_ref, m2m_ref, out_ref, moved, *sums):
    points, box_count = fine_ref.shape
    clear(sums)

    def translate(step, carry):
        first = pl.multiple_of(step * CHUNK, CHUNK)
        columns = fine_ref[:, pl.ds(first, CHUNK)]
        octants = octant_ref[:, pl.ds(first, CHUNK)]
        total = jnp.zeros((points, CHUNK), jnp.float32)
        for octant in range(8):
            shifted = jnp.dot(m2m_ref[octant], columns, preferred_element_type=jnp.float32)
            total = total + jnp.where(octants == octant, shifted, jnp.float32(0.0))
        rows_to_pairs(total.T, moved, first, CHUNK)
        return carry

    lax.fori_loop(0, box_count // CHUNK, translate, 0)
    unroll = 64

    def scatter(step, carry):
        base = step * unroll
        first = pl.multiple_of(2 * base, 2 * unroll)
        for k in range(0, unroll, MERGE_COPIES):
            at = [pl.multiple_of(slot_ref[0, base + k + c], 2) for c in range(MERGE_COPIES)]
            new = [
                sums[c][pl.ds(at[c], 2), :] + moved[pl.ds(first + 2 * (k + c), 2), :]
                for c in range(MERGE_COPIES)
            ]
            for c in range(MERGE_COPIES):
                sums[c][pl.ds(at[c], 2), :] = new[c]
        return carry

    lax.fori_loop(0, box_count // unroll, scatter, 0)
    pairs_to_columns(sums, out_ref)


def merge_upward(fine_density, m2m_ops, parent_slot, octant, parent_count):
    points, box_count = fine_density.shape
    vmem = pl.BlockSpec(memory_space=pltpu.VMEM)
    return pl.pallas_call(
        merge_kernel,
        in_specs=[pl.BlockSpec(memory_space=pltpu.SMEM), vmem, vmem, vmem],
        out_specs=vmem,
        out_shape=jax.ShapeDtypeStruct((points, parent_count), jnp.float32),
        scratch_shapes=[pltpu.VMEM((2 * box_count, LANES), jnp.float32)]
        + [pltpu.VMEM((2 * parent_count, LANES), jnp.float32)] * MERGE_COPIES,
        compiler_params=pltpu.CompilerParams(vmem_limit_bytes=VMEM_LIMIT),
        name="merge_upward",
    )((2 * parent_slot)[None, :], octant[None, :], fine_density, m2m_ops)


def translate_kernel(slots, op_ref, index_hbm, fine_ref, blocks_hbm, *refs):
    ops, refs = refs[:GROUP], refs[GROUP:]
    out_ref, refs = refs[0], refs[1:]
    table, landed, landed_sem, refs = refs[0], refs[1:3], refs[3], refs[4:]
    gathered, refs = refs[:2], refs[2:]
    products, refs = refs[:2], refs[2:]
    index, refs = refs[:GROUP], refs[GROUP:]
    sem, totals = refs[0], refs[1:]
    step, steps = pl.program_id(0), pl.num_programs(0)
    points, box_count = fine_ref.shape

    def index_copy(which, batch):
        return pltpu.make_async_copy(index_hbm.at[batch], index[which], sem.at[which])

    @pl.when(step == 0)
    def _():
        for which in range(GROUP):
            index_copy(which, which).start()
        clear(gathered)
        clear(products)
        clear(totals)
        peers, packed, _ = blocks_hbm.shape
        capacity = packed // (PARTS + 1) * PARTS
        quarter = capacity // PARTS
        lane = lax.broadcasted_iota(jnp.int32, (quarter, LANES), 1)

        def block_copy(peer, slot):
            return pltpu.make_async_copy(blocks_hbm.at[peer], landed[slot], landed_sem.at[slot])

        for slot in range(2):
            block_copy(slot, slot).start()
        clear(gathered)
        clear(products)
        clear(totals)
        columns_to_pairs(fine_ref, table)

        def unpack(peer, block):
            tails = block[pl.ds(capacity, quarter), :].astype(jnp.float32)
            for part in range(PARTS):
                first = pl.multiple_of(2 * (box_count + peer * capacity), 2 * quarter)
                first = first + 2 * part * quarter
                head = block[pl.ds(part * quarter, quarter), :]
                tail = pltpu.roll(tails, (PARTS - part) * (LANES // PARTS), 1) if part else tails
                tail = jnp.where(lane < points - LANES, tail, jnp.float32(0.0))
                table[pl.ds(first, quarter, stride=2), :] = head.astype(jnp.float32)
                table[pl.ds(first + 1, quarter, stride=2), :] = tail

        def unpack_two(pair, carry):
            for slot in range(2):
                peer = 2 * pair + slot
                block_copy(peer, slot).wait()
                unpack(peer, landed[slot])

                @pl.when(pair < peers // 2 - 1)
                def _():
                    block_copy(peer + 2, slot).start()

            return carry

        lax.fori_loop(0, peers // 2, unpack_two, 0)

    for which in range(GROUP):
        now, before = which % 2, 1 - which % 2
        if which % SPAN == 0:
            for each in range(which, which + SPAN):
                index_copy(each, step * GROUP + each).wait()
        columns = jnp.concatenate(
            [
                gathered[before][pl.ds(0, slots, stride=2), :],
                gathered[before][pl.ds(1, slots, stride=2), :],
            ],
            axis=1,
        )[:, :points].astype(jnp.bfloat16)
        product = lax.dot_general(
            columns, ops[which][0], (((1,), (1,)), ((), ())), preferred_element_type=jnp.float32
        )
        products[before][pl.ds(0, slots, stride=2), :] = product[:, :LANES]
        products[before][pl.ds(1, slots, stride=2), pl.ds(0, points - LANES)] = product[:, LANES:]
        for k in range(0, slots, COPIES):
            at = [pl.multiple_of(index[which][0, slots + k + c], 2) for c in range(COPIES)]
            new = [
                totals[c][pl.ds(at[c], 2), :] + products[now][pl.ds(2 * (k + c), 2), :]
                for c in range(COPIES)
            ]
            for c in range(COPIES):
                totals[c][pl.ds(at[c], 2), :] = new[c]
            for c in range(COPIES):
                row = pl.multiple_of(index[which][0, k + c], 2)
                gathered[now][pl.ds(2 * (k + c), 2), :] = table[pl.ds(row, 2), :]
        if which % SPAN == SPAN - 1:
            for each in range(which - SPAN + 1, which + 1):
                index_copy(each, (step + 1) * GROUP + each).start()

    @pl.when(step == steps - 1)
    def _():
        for which in range(GROUP):
            index_copy(which, (step + 1) * GROUP + which).wait()
        pairs_to_columns(totals, out_ref)


def translate_lists(fine_density, blocks, m2l_ops, batch_op, source_entry, target):
    points, box_count = fine_density.shape
    batches, slots = source_entry.shape
    peers, packed, _ = blocks.shape
    capacity = packed // (PARTS + 1) * PARTS
    steps = -(-(batches + 2) // GROUP)
    padded = (steps + 1) * GROUP
    source = jnp.pad(2 * source_entry, ((0, padded - batches), (0, 0)))
    target = jnp.pad(
        2 * target, ((2, padded - batches - 2), (0, 0)), constant_values=2 * box_count
    )
    index = jnp.concatenate([source, target], axis=1)[:, None, :]
    op_index = jnp.pad(batch_op, (1, padded - batches - 1))
    vmem = pl.BlockSpec(memory_space=pltpu.VMEM)
    operators = [
        pl.BlockSpec((1, points, points), lambda j, ops, which=which: (ops[j * GROUP + which], 0, 0))
        for which in range(GROUP)
    ]
    return pl.pallas_call(
        functools.partial(translate_kernel, slots),
        grid_spec=pltpu.PrefetchScalarGridSpec(
            num_scalar_prefetch=1,
            grid=(steps,),
            in_specs=[pl.BlockSpec(memory_space=pl.ANY), vmem, pl.BlockSpec(memory_space=pl.ANY)] + operators,
            out_specs=vmem,
            scratch_shapes=[pltpu.VMEM((2 * (box_count + peers * capacity), LANES), jnp.float32)]
            + [pltpu.VMEM((packed, LANES), jnp.bfloat16)] * 2
            + [pltpu.SemaphoreType.DMA((2,))]
            + [pltpu.VMEM((2 * slots, LANES), jnp.float32)] * 4
            + [pltpu.SMEM((1, 2 * slots), jnp.int32)] * GROUP
            + [pltpu.SemaphoreType.DMA((GROUP,))]
            + [pltpu.VMEM((2 * (box_count + 8), LANES), jnp.float32)] * COPIES,
        ),
        out_shape=jax.ShapeDtypeStruct((points, box_count), jnp.float32),
        compiler_params=pltpu.CompilerParams(
            vmem_limit_bytes=VMEM_LIMIT, dimension_semantics=("arbitrary",)
        ),
        name="translate_lists",
    )(op_index, index, fine_density, blocks, *[m2l_ops] * GROUP)


def per_device(
    fine_density,
    m2m_ops,
    m2l_ops,
    parent_slot,
    octant,
    send_rows,
    batch_op,
    batch_source_entry,
    batch_tgt,
):
    points, box_count = fine_density.shape
    parent_count = box_count // 4 * lax.axis_size("leaf")
    blocks = pack_blocks(fine_density, send_rows)
    merge_density, blocks = lax.optimization_barrier((fine_density, blocks))
    blocks = lax.all_to_all(blocks, "space", 0, 0, tiled=True)
    partial_sums = merge_upward(merge_density, m2m_ops, parent_slot, octant, parent_count)
    coarse_level = lax.psum_scatter(partial_sums, "leaf", scatter_dimension=1, tiled=True)
    local_coeffs = translate_lists(
        fine_density, blocks, m2l_ops, batch_op, batch_source_entry, batch_tgt
    )
    return (local_coeffs, coarse_level[:, None, :])


def solution(mesh):
    return jax.shard_map(
        per_device,
        mesh=mesh,
        in_specs=(
            P(None, ("leaf", "space")),
            P(),
            P(),
            P(("leaf", "space")),
            P(("leaf", "space")),
            P(("leaf", "space"), None),
            P(("leaf", "space")),
            P(("leaf", "space"), None),
            P(("leaf", "space"), None),
        ),
        out_specs=(P(None, ("leaf", "space")), P(None, "space", "leaf")),
        check_vma=False,
    )
```

```python
import functools

import jax
import jax.numpy as jnp
from jax import lax
from jax.experimental import pallas as pl
from jax.experimental.pallas import tpu as pltpu
from jax.sharding import PartitionSpec as P

LANES = 128
CHUNK = 256
GROUP = 4
SPAN = 1
COPIES = 8
MERGE_COPIES = 4
PARTS = 4
VMEM_LIMIT = 62 * 2**20


def rows_to_pairs(values, ref, first, count):
    points = values.shape[1]
    tail = jnp.concatenate(
        [values[:, LANES:], jnp.zeros((count, 2 * LANES - points), values.dtype)], axis=1
    )
    ref[pl.ds(2 * first, count, stride=2), :] = values[:, :LANES]
    ref[pl.ds(2 * first + 1, count, stride=2), :] = tail


def columns_to_pairs(columns_ref, ref):
    points, count = columns_ref.shape

    def body(step, carry):
        first = pl.multiple_of(step * CHUNK, CHUNK)
        columns = columns_ref[:, pl.ds(first, CHUNK)].astype(jnp.float32)
        rows_to_pairs(columns.T, ref, first, CHUNK)
        return carry

    lax.fori_loop(0, count // CHUNK, body, 0)


def pairs_to_columns(refs, out_ref):
    points, count = out_ref.shape

    def body(step, carry):
        first = pl.multiple_of(step * CHUNK, CHUNK)
        head = refs[0][pl.ds(2 * first, CHUNK, stride=2), :]
        tail = refs[0][pl.ds(2 * first + 1, CHUNK, stride=2), :]
        for ref in refs[1:]:
            head = head + ref[pl.ds(2 * first, CHUNK, stride=2), :]
            tail = tail + ref[pl.ds(2 * first + 1, CHUNK, stride=2), :]
        out_ref[pl.ds(0, LANES), pl.ds(first, CHUNK)] = head.T
        out_ref[pl.ds(LANES, points - LANES), pl.ds(first, CHUNK)] = tail.T[: points - LANES]
        return carry

    lax.fori_loop(0, count // CHUNK, body, 0)


def clear(refs):
    def body(step, carry):
        for ref in refs:
            ref[pl.ds(pl.multiple_of(step * 16, 16), 16), :] = jnp.zeros((16, LANES), ref.dtype)
        return carry

    lax.fori_loop(0, refs[0].shape[0] // 16, body, 0)


def pack_kernel(rows_ref, fine_ref, out_ref, table, staged):
    @pl.when(pl.program_id(0) == 0)
    def _():
        columns_to_pairs(fine_ref, table)

    capacity = rows_ref.shape[2]
    unroll = 128

    def gather(step, carry):
        base = step * unroll
        for k in range(unroll):
            row = pl.multiple_of(rows_ref[0, 0, base + k], 2)
            staged[pl.ds(pl.multiple_of(2 * base, 2 * unroll) + 2 * k, 2), :] = table[pl.ds(row, 2), :]
        return carry

    lax.fori_loop(0, capacity // unroll, gather, 0)
    quarter = capacity // PARTS
    tails = staged[pl.ds(1, quarter, stride=2), :]
    for part in range(PARTS):
        start = 2 * part * quarter
        out_ref[0, pl.ds(part * quarter, quarter), :] = staged[
            pl.ds(start, quarter, stride=2), :
        ].astype(jnp.bfloat16)
        if part:
            tail = staged[pl.ds(start + 1, quarter, stride=2), :]
            tails = tails + pltpu.roll(tail, part * (LANES // PARTS), 1)
    out_ref[0, pl.ds(capacity, quarter), :] = tails.astype(jnp.bfloat16)


def pack_blocks(fine_density, send_rows):
    points, box_count = fine_density.shape
    peers, capacity = send_rows.shape
    packed = capacity + capacity // PARTS
    return pl.pallas_call(
        pack_kernel,
        grid=(peers,),
        in_specs=[
            pl.BlockSpec((1, 1, capacity), lambda q: (q, 0, 0), memory_space=pltpu.SMEM),
            pl.BlockSpec(memory_space=pltpu.VMEM),
        ],
        out_specs=pl.BlockSpec((1, packed, LANES), lambda q: (q, 0, 0)),
        out_shape=jax.ShapeDtypeStruct((peers, packed, LANES), jnp.bfloat16),
        scratch_shapes=[
            pltpu.VMEM((2 * box_count, LANES), jnp.float32),
            pltpu.VMEM((2 * capacity, LANES), jnp.float32),
        ],
        compiler_params=pltpu.CompilerParams(vmem_limit_bytes=VMEM_LIMIT),
        name="pack_blocks",
    )((2 * send_rows)[:, None, :], fine_density)


def merge_kernel(slot_ref, octant_ref, fine_ref, m2m_ref, after_hbm, out_ref, moved, *sums):
    del after_hbm
    points, box_count = fine_ref.shape
    clear(sums)

    def translate(step, carry):
        first = pl.multiple_of(step * CHUNK, CHUNK)
        columns = fine_ref[:, pl.ds(first, CHUNK)]
        octants = octant_ref[:, pl.ds(first, CHUNK)]
        total = jnp.zeros((points, CHUNK), jnp.float32)
        for octant in range(8):
            shifted = jnp.dot(m2m_ref[octant], columns, preferred_element_type=jnp.float32)
            total = total + jnp.where(octants == octant, shifted, jnp.float32(0.0))
        rows_to_pairs(total.T, moved, first, CHUNK)
        return carry

    lax.fori_loop(0, box_count // CHUNK, translate, 0)
    unroll = 64

    def scatter(step, carry):
        base = step * unroll
        first = pl.multiple_of(2 * base, 2 * unroll)
        for k in range(0, unroll, MERGE_COPIES):
            at = [pl.multiple_of(slot_ref[0, base + k + c], 2) for c in range(MERGE_COPIES)]
            new = [
                sums[c][pl.ds(at[c], 2), :] + moved[pl.ds(first + 2 * (k + c), 2), :]
                for c in range(MERGE_COPIES)
            ]
            for c in range(MERGE_COPIES):
                sums[c][pl.ds(at[c], 2), :] = new[c]
        return carry

    lax.fori_loop(0, box_count // unroll, scatter, 0)
    pairs_to_columns(sums, out_ref)


def merge_upward(fine_density, m2m_ops, parent_slot, octant, parent_count, after):
    points, box_count = fine_density.shape
    vmem = pl.BlockSpec(memory_space=pltpu.VMEM)
    return pl.pallas_call(
        merge_kernel,
        in_specs=[pl.BlockSpec(memory_space=pltpu.SMEM), vmem, vmem, vmem, pl.BlockSpec(memory_space=pl.ANY)],
        out_specs=vmem,
        out_shape=jax.ShapeDtypeStruct((points, parent_count), jnp.float32),
        scratch_shapes=[pltpu.VMEM((2 * box_count, LANES), jnp.float32)]
        + [pltpu.VMEM((2 * parent_count, LANES), jnp.float32)] * MERGE_COPIES,
        compiler_params=pltpu.CompilerParams(vmem_limit_bytes=VMEM_LIMIT),
        name="merge_upward",
    )((2 * parent_slot)[None, :], octant[None, :], fine_density, m2m_ops, after)


def translate_kernel(slots, op_ref, index_hbm, fine_ref, blocks_hbm, *refs):
    ops, refs = refs[:GROUP], refs[GROUP:]
    out_ref, refs = refs[0], refs[1:]
    table, landed, landed_sem, refs = refs[0], refs[1:3], refs[3], refs[4:]
    gathered, refs = refs[:2], refs[2:]
    products, refs = refs[:2], refs[2:]
    index, refs = refs[:GROUP], refs[GROUP:]
    sem, totals = refs[0], refs[1:]
    step, steps = pl.program_id(0), pl.num_programs(0)
    points, box_count = fine_ref.shape

    def index_copy(which, batch):
        return pltpu.make_async_copy(index_hbm.at[batch], index[which], sem.at[which])

    @pl.when(step == 0)
    def _():
        for which in range(GROUP):
            index_copy(which, which).start()
        clear(gathered)
        clear(products)
        clear(totals)
        peers, packed, _ = blocks_hbm.shape
        capacity = packed // (PARTS + 1) * PARTS
        quarter = capacity // PARTS
        lane = lax.broadcasted_iota(jnp.int32, (quarter, LANES), 1)

        def block_copy(peer, slot):
            return pltpu.make_async_copy(blocks_hbm.at[peer], landed[slot], landed_sem.at[slot])

        for slot in range(2):
            block_copy(slot, slot).start()
        clear(gathered)
        clear(products)
        clear(totals)
        columns_to_pairs(fine_ref, table)

        def unpack(peer, block):
            tails = block[pl.ds(capacity, quarter), :].astype(jnp.float32)
            for part in range(PARTS):
                first = pl.multiple_of(2 * (box_count + peer * capacity), 2 * quarter)
                first = first + 2 * part * quarter
                head = block[pl.ds(part * quarter, quarter), :]
                tail = pltpu.roll(tails, (PARTS - part) * (LANES // PARTS), 1) if part else tails
                tail = jnp.where(lane < points - LANES, tail, jnp.float32(0.0))
                table[pl.ds(first, quarter, stride=2), :] = head.astype(jnp.float32)
                table[pl.ds(first + 1, quarter, stride=2), :] = tail

        def unpack_two(pair, carry):
            for slot in range(2):
                peer = 2 * pair + slot
                block_copy(peer, slot).wait()
                unpack(peer, landed[slot])

                @pl.when(pair < peers // 2 - 1)
                def _():
                    block_copy(peer + 2, slot).start()

            return carry

        lax.fori_loop(0, peers // 2, unpack_two, 0)

    for which in range(GROUP):
        now, before = which % 2, 1 - which % 2
        if which % SPAN == 0:
            for each in range(which, which + SPAN):
                index_copy(each, step * GROUP + each).wait()
        columns = jnp.concatenate(
            [
                gathered[before][pl.ds(0, slots, stride=2), :],
                gathered[before][pl.ds(1, slots, stride=2), :],
            ],
            axis=1,
        )[:, :points].astype(jnp.bfloat16)
        product = lax.dot_general(
            columns, ops[which][0], (((1,), (1,)), ((), ())), preferred_element_type=jnp.float32
        )
        products[before][pl.ds(0, slots, stride=2), :] = product[:, :LANES]
        products[before][pl.ds(1, slots, stride=2), pl.ds(0, points - LANES)] = product[:, LANES:]
        for k in range(0, slots, COPIES):
            at = [pl.multiple_of(index[which][0, slots + k + c], 2) for c in range(COPIES)]
            new = [
                totals[c][pl.ds(at[c], 2), :] + products[now][pl.ds(2 * (k + c), 2), :]
                for c in range(COPIES)
            ]
            for c in range(COPIES):
                totals[c][pl.ds(at[c], 2), :] = new[c]
            for c in range(COPIES):
                row = pl.multiple_of(index[which][0, k + c], 2)
                gathered[now][pl.ds(2 * (k + c), 2), :] = table[pl.ds(row, 2), :]
        if which % SPAN == SPAN - 1:
            for each in range(which - SPAN + 1, which + 1):
                index_copy(each, (step + 1) * GROUP + each).start()

    @pl.when(step == steps - 1)
    def _():
        for which in range(GROUP):
            index_copy(which, (step + 1) * GROUP + which).wait()
        pairs_to_columns(totals, out_ref)


def translate_lists(fine_density, blocks, m2l_ops, batch_op, source_entry, target):
    points, box_count = fine_density.shape
    batches, slots = source_entry.shape
    peers, packed, _ = blocks.shape
    capacity = packed // (PARTS + 1) * PARTS
    steps = -(-(batches + 2) // GROUP)
    padded = (steps + 1) * GROUP
    source = jnp.pad(2 * source_entry, ((0, padded - batches), (0, 0)))
    target = jnp.pad(
        2 * target, ((2, padded - batches - 2), (0, 0)), constant_values=2 * box_count
    )
    index = jnp.concatenate([source, target], axis=1)[:, None, :]
    op_index = jnp.pad(batch_op, (1, padded - batches - 1))
    vmem = pl.BlockSpec(memory_space=pltpu.VMEM)
    operators = [
        pl.BlockSpec((1, points, points), lambda j, ops, which=which: (ops[j * GROUP + which], 0, 0))
        for which in range(GROUP)
    ]
    return pl.pallas_call(
        functools.partial(translate_kernel, slots),
        grid_spec=pltpu.PrefetchScalarGridSpec(
            num_scalar_prefetch=1,
            grid=(steps,),
            in_specs=[pl.BlockSpec(memory_space=pl.ANY), vmem, pl.BlockSpec(memory_space=pl.ANY)] + operators,
            out_specs=vmem,
            scratch_shapes=[pltpu.VMEM((2 * (box_count + peers * capacity), LANES), jnp.float32)]
            + [pltpu.VMEM((packed, LANES), jnp.bfloat16)] * 2
            + [pltpu.SemaphoreType.DMA((2,))]
            + [pltpu.VMEM((2 * slots, LANES), jnp.float32)] * 4
            + [pltpu.SMEM((1, 2 * slots), jnp.int32)] * GROUP
            + [pltpu.SemaphoreType.DMA((GROUP,))]
            + [pltpu.VMEM((2 * (box_count + 8), LANES), jnp.float32)] * COPIES,
        ),
        out_shape=jax.ShapeDtypeStruct((points, box_count), jnp.float32),
        compiler_params=pltpu.CompilerParams(
            vmem_limit_bytes=VMEM_LIMIT, dimension_semantics=("arbitrary",)
        ),
        cost_estimate=pl.CostEstimate(
            flops=2 * batches * slots * points**2,
            bytes_accessed=batches * slots * 12 * LANES * 4,
            transcendentals=0,
        ),
        name="translate_lists",
    )(op_index, index, fine_density, blocks, *[m2l_ops] * GROUP)


def per_device(
    fine_density,
    m2m_ops,
    m2l_ops,
    parent_slot,
    octant,
    send_rows,
    batch_op,
    batch_source_entry,
    batch_tgt,
):
    points, box_count = fine_density.shape
    parent_count = box_count // 4 * lax.axis_size("leaf")
    blocks = pack_blocks(fine_density, send_rows)
    merge_density, blocks = lax.optimization_barrier((fine_density, blocks))
    blocks = lax.all_to_all(blocks, "space", 0, 0, tiled=True)
    partial_sums = merge_upward(
        merge_density, m2m_ops, parent_slot, octant, parent_count, after=m2l_ops
    )
    partial_sums, blocks = lax.optimization_barrier((partial_sums, blocks))
    coarse_level = lax.psum_scatter(partial_sums, "leaf", scatter_dimension=1, tiled=True)
    local_coeffs = translate_lists(
        fine_density, blocks, m2l_ops, batch_op, batch_source_entry, batch_tgt
    )
    return (local_coeffs, coarse_level[:, None, :])


def solution(mesh):
    return jax.shard_map(
        per_device,
        mesh=mesh,
        in_specs=(
            P(None, ("leaf", "space")),
            P(),
            P(),
            P(("leaf", "space")),
            P(("leaf", "space")),
            P(("leaf", "space"), None),
            P(("leaf", "space")),
            P(("leaf", "space"), None),
            P(("leaf", "space"), None),
        ),
        out_specs=(P(None, ("leaf", "space")), P(None, "space", "leaf")),
        check_vma=False,
    )
```

```python
import functools

import jax
import jax.numpy as jnp
from jax import lax
from jax.experimental import pallas as pl
from jax.experimental.pallas import tpu as pltpu
from jax.sharding import PartitionSpec as P

LANES = 128
CHUNK = 256
GROUP = 4
SPAN = 1
COPIES = 8
MERGE_COPIES = 4
PARTS = 4
VMEM_LIMIT = 62 * 2**20


def rows_to_pairs(values, ref, first, count):
    points = values.shape[1]
    tail = jnp.concatenate(
        [values[:, LANES:], jnp.zeros((count, 2 * LANES - points), values.dtype)], axis=1
    )
    ref[pl.ds(2 * first, count, stride=2), :] = values[:, :LANES]
    ref[pl.ds(2 * first + 1, count, stride=2), :] = tail


def columns_to_pairs(columns_ref, ref):
    points, count = columns_ref.shape

    def body(step, carry):
        first = pl.multiple_of(step * CHUNK, CHUNK)
        columns = columns_ref[:, pl.ds(first, CHUNK)].astype(jnp.float32)
        rows_to_pairs(columns.T, ref, first, CHUNK)
        return carry

    lax.fori_loop(0, count // CHUNK, body, 0)


def pairs_to_columns(refs, out_ref):
    points, count = out_ref.shape

    def body(step, carry):
        first = pl.multiple_of(step * CHUNK, CHUNK)
        head = refs[0][pl.ds(2 * first, CHUNK, stride=2), :]
        tail = refs[0][pl.ds(2 * first + 1, CHUNK, stride=2), :]
        for ref in refs[1:]:
            head = head + ref[pl.ds(2 * first, CHUNK, stride=2), :]
            tail = tail + ref[pl.ds(2 * first + 1, CHUNK, stride=2), :]
        out_ref[pl.ds(0, LANES), pl.ds(first, CHUNK)] = head.T
        out_ref[pl.ds(LANES, points - LANES), pl.ds(first, CHUNK)] = tail.T[: points - LANES]
        return carry

    lax.fori_loop(0, count // CHUNK, body, 0)


def clear(refs):
    def body(step, carry):
        for ref in refs:
            ref[pl.ds(pl.multiple_of(step * 16, 16), 16), :] = jnp.zeros((16, LANES), ref.dtype)
        return carry

    lax.fori_loop(0, refs[0].shape[0] // 16, body, 0)


def pack_kernel(rows_ref, fine_ref, out_ref, table, staged):
    @pl.when(pl.program_id(0) == 0)
    def _():
        columns_to_pairs(fine_ref, table)

    capacity = rows_ref.shape[2]
    unroll = 128

    def gather(step, carry):
        base = step * unroll
        for k in range(unroll):
            row = pl.multiple_of(rows_ref[0, 0, base + k], 2)
            staged[pl.ds(pl.multiple_of(2 * base, 2 * unroll) + 2 * k, 2), :] = table[pl.ds(row, 2), :]
        return carry

    lax.fori_loop(0, capacity // unroll, gather, 0)
    quarter = capacity // PARTS
    tails = staged[pl.ds(1, quarter, stride=2), :]
    for part in range(PARTS):
        start = 2 * part * quarter
        out_ref[0, pl.ds(part * quarter, quarter), :] = staged[
            pl.ds(start, quarter, stride=2), :
        ].astype(jnp.bfloat16)
        if part:
            tail = staged[pl.ds(start + 1, quarter, stride=2), :]
            tails = tails + pltpu.roll(tail, part * (LANES // PARTS), 1)
    out_ref[0, pl.ds(capacity, quarter), :] = tails.astype(jnp.bfloat16)


def pack_blocks(fine_density, send_rows):
    points, box_count = fine_density.shape
    peers, capacity = send_rows.shape
    packed = capacity + capacity // PARTS
    return pl.pallas_call(
        pack_kernel,
        grid=(peers,),
        in_specs=[
            pl.BlockSpec((1, 1, capacity), lambda q: (q, 0, 0), memory_space=pltpu.SMEM),
            pl.BlockSpec(memory_space=pltpu.VMEM),
        ],
        out_specs=pl.BlockSpec((1, packed, LANES), lambda q: (q, 0, 0)),
        out_shape=jax.ShapeDtypeStruct((peers, packed, LANES), jnp.bfloat16),
        scratch_shapes=[
            pltpu.VMEM((2 * box_count, LANES), jnp.float32),
            pltpu.VMEM((2 * capacity, LANES), jnp.float32),
        ],
        compiler_params=pltpu.CompilerParams(vmem_limit_bytes=VMEM_LIMIT),
        name="pack_blocks",
    )((2 * send_rows)[:, None, :], fine_density)


def merge_kernel(slot_ref, octant_ref, fine_ref, m2m_ref, after_hbm, out_ref, moved, *sums):
    del after_hbm
    points, box_count = fine_ref.shape
    clear(sums)

    def translate(step, carry):
        first = pl.multiple_of(step * CHUNK, CHUNK)
        columns = fine_ref[:, pl.ds(first, CHUNK)]
        octants = octant_ref[:, pl.ds(first, CHUNK)]
        total = jnp.zeros((points, CHUNK), jnp.float32)
        for octant in range(8):
            shifted = jnp.dot(m2m_ref[octant], columns, preferred_element_type=jnp.float32)
            total = total + jnp.where(octants == octant, shifted, jnp.float32(0.0))
        rows_to_pairs(total.T, moved, first, CHUNK)
        return carry

    lax.fori_loop(0, box_count // CHUNK, translate, 0)
    unroll = 64

    def scatter(step, carry):
        base = step * unroll
        first = pl.multiple_of(2 * base, 2 * unroll)
        for k in range(0, unroll, MERGE_COPIES):
            at = [pl.multiple_of(slot_ref[0, base + k + c], 2) for c in range(MERGE_COPIES)]
            new = [
                sums[c][pl.ds(at[c], 2), :] + moved[pl.ds(first + 2 * (k + c), 2), :]
                for c in range(MERGE_COPIES)
            ]
            for c in range(MERGE_COPIES):
                sums[c][pl.ds(at[c], 2), :] = new[c]
        return carry

    lax.fori_loop(0, box_count // unroll, scatter, 0)
    pairs_to_columns(sums, out_ref)


def merge_upward(fine_density, m2m_ops, parent_slot, octant, parent_count, after):
    points, box_count = fine_density.shape
    vmem = pl.BlockSpec(memory_space=pltpu.VMEM)
    return pl.pallas_call(
        merge_kernel,
        in_specs=[pl.BlockSpec(memory_space=pltpu.SMEM), vmem, vmem, vmem, pl.BlockSpec(memory_space=pl.ANY)],
        out_specs=vmem,
        out_shape=jax.ShapeDtypeStruct((points, parent_count), jnp.float32),
        scratch_shapes=[pltpu.VMEM((2 * box_count, LANES), jnp.float32)]
        + [pltpu.VMEM((2 * parent_count, LANES), jnp.float32)] * MERGE_COPIES,
        compiler_params=pltpu.CompilerParams(vmem_limit_bytes=VMEM_LIMIT),
        name="merge_upward",
    )((2 * parent_slot)[None, :], octant[None, :], fine_density, m2m_ops, after)


def translate_kernel(slots, op_ref, index_hbm, fine_ref, blocks_hbm, *refs):
    ops, refs = refs[:GROUP], refs[GROUP:]
    out_ref, refs = refs[0], refs[1:]
    table, landed, landed_sem, refs = refs[0], refs[1:3], refs[3], refs[4:]
    gathered, refs = refs[:2], refs[2:]
    products, refs = refs[:2], refs[2:]
    index, refs = refs[:GROUP], refs[GROUP:]
    sem, totals = refs[0], refs[1:]
    step, steps = pl.program_id(0), pl.num_programs(0)
    points, box_count = fine_ref.shape

    def index_copy(which, batch):
        return pltpu.make_async_copy(index_hbm.at[batch], index[which], sem.at[which])

    @pl.when(step == 0)
    def _():
        for which in range(GROUP):
            index_copy(which, which).start()
        clear(gathered)
        clear(products)
        clear(totals)
        peers, packed, _ = blocks_hbm.shape
        capacity = packed // (PARTS + 1) * PARTS
        quarter = capacity // PARTS
        lane = lax.broadcasted_iota(jnp.int32, (quarter, LANES), 1)

        def block_copy(peer, slot):
            return pltpu.make_async_copy(blocks_hbm.at[peer], landed[slot], landed_sem.at[slot])

        for slot in range(2):
            block_copy(slot, slot).start()
        clear(gathered)
        clear(products)
        clear(totals)
        columns_to_pairs(fine_ref, table)

        def unpack(peer, block):
            tails = block[pl.ds(capacity, quarter), :].astype(jnp.float32)
            for part in range(PARTS):
                first = pl.multiple_of(2 * (box_count + peer * capacity), 2 * quarter)
                first = first + 2 * part * quarter
                head = block[pl.ds(part * quarter, quarter), :]
                tail = pltpu.roll(tails, (PARTS - part) * (LANES // PARTS), 1) if part else tails
                tail = jnp.where(lane < points - LANES, tail, jnp.float32(0.0))
                table[pl.ds(first, quarter, stride=2), :] = head.astype(jnp.float32)
                table[pl.ds(first + 1, quarter, stride=2), :] = tail

        def unpack_two(pair, carry):
            for slot in range(2):
                peer = 2 * pair + slot
                block_copy(peer, slot).wait()
                unpack(peer, landed[slot])

                @pl.when(pair < peers // 2 - 1)
                def _():
                    block_copy(peer + 2, slot).start()

            return carry

        lax.fori_loop(0, peers // 2, unpack_two, 0)

    for which in range(GROUP):
        now, before = which % 2, 1 - which % 2
        if which % SPAN == 0:
            for each in range(which, which + SPAN):
                index_copy(each, step * GROUP + each).wait()
        columns = jnp.concatenate(
            [
                gathered[before][pl.ds(0, slots, stride=2), :],
                gathered[before][pl.ds(1, slots, stride=2), :],
            ],
            axis=1,
        )[:, :points].astype(jnp.bfloat16)
        product = lax.dot_general(
            columns, ops[which][0], (((1,), (1,)), ((), ())), preferred_element_type=jnp.float32
        )
        products[before][pl.ds(0, slots, stride=2), :] = product[:, :LANES]
        products[before][pl.ds(1, slots, stride=2), pl.ds(0, points - LANES)] = product[:, LANES:]
        for k in range(0, slots, COPIES):
            at = [pl.multiple_of(index[which][0, slots + k + c], 2) for c in range(COPIES)]
            new = [
                totals[c][pl.ds(at[c], 2), :] + products[now][pl.ds(2 * (k + c), 2), :]
                for c in range(COPIES)
            ]
            for c in range(COPIES):
                totals[c][pl.ds(at[c], 2), :] = new[c]
            for c in range(COPIES):
                row = pl.multiple_of(index[which][0, k + c], 2)
                gathered[now][pl.ds(2 * (k + c), 2), :] = table[pl.ds(row, 2), :]
        if which % SPAN == SPAN - 1:
            for each in range(which - SPAN + 1, which + 1):
                index_copy(each, (step + 1) * GROUP + each).start()

    @pl.when(step == steps - 1)
    def _():
        for which in range(GROUP):
            index_copy(which, (step + 1) * GROUP + which).wait()
        pairs_to_columns(totals, out_ref)


def slot_indices(batch_op, source_entry, target, box_count):
    batches, slots = source_entry.shape
    steps = -(-(batches + 2) // GROUP)
    padded = (steps + 1) * GROUP
    source = jnp.pad(2 * source_entry, ((0, padded - batches), (0, 0)))
    target = jnp.pad(
        2 * target, ((2, padded - batches - 2), (0, 0)), constant_values=2 * box_count
    )
    index = jnp.concatenate([source, target], axis=1)[:, None, :]
    return index, jnp.pad(batch_op, (1, padded - batches - 1))


def translate_lists(fine_density, blocks, m2l_ops, index, op_index):
    points, box_count = fine_density.shape
    padded, _, slots = index.shape
    slots = slots // 2
    steps = padded // GROUP - 1
    batches = steps * GROUP
    peers, packed, _ = blocks.shape
    capacity = packed // (PARTS + 1) * PARTS
    vmem = pl.BlockSpec(memory_space=pltpu.VMEM)
    operators = [
        pl.BlockSpec((1, points, points), lambda j, ops, which=which: (ops[j * GROUP + which], 0, 0))
        for which in range(GROUP)
    ]
    return pl.pallas_call(
        functools.partial(translate_kernel, slots),
        grid_spec=pltpu.PrefetchScalarGridSpec(
            num_scalar_prefetch=1,
            grid=(steps,),
            in_specs=[pl.BlockSpec(memory_space=pl.ANY), vmem, pl.BlockSpec(memory_space=pl.ANY)] + operators,
            out_specs=vmem,
            scratch_shapes=[pltpu.VMEM((2 * (box_count + peers * capacity), LANES), jnp.float32)]
            + [pltpu.VMEM((packed, LANES), jnp.bfloat16)] * 2
            + [pltpu.SemaphoreType.DMA((2,))]
            + [pltpu.VMEM((2 * slots, LANES), jnp.float32)] * 4
            + [pltpu.SMEM((1, 2 * slots), jnp.int32)] * GROUP
            + [pltpu.SemaphoreType.DMA((GROUP,))]
            + [pltpu.VMEM((2 * (box_count + 8), LANES), jnp.float32)] * COPIES,
        ),
        out_shape=jax.ShapeDtypeStruct((points, box_count), jnp.float32),
        compiler_params=pltpu.CompilerParams(
            vmem_limit_bytes=VMEM_LIMIT, dimension_semantics=("arbitrary",)
        ),
        cost_estimate=pl.CostEstimate(
            flops=2 * batches * slots * points**2,
            bytes_accessed=batches * slots * 12 * LANES * 4,
            transcendentals=0,
        ),
        name="translate_lists",
    )(op_index, index, fine_density, blocks, *[m2l_ops] * GROUP)


def per_device(
    fine_density,
    m2m_ops,
    m2l_ops,
    parent_slot,
    octant,
    send_rows,
    batch_op,
    batch_source_entry,
    batch_tgt,
):
    points, box_count = fine_density.shape
    parent_count = box_count // 4 * lax.axis_size("leaf")
    blocks = pack_blocks(fine_density, send_rows)
    index, op_index = slot_indices(batch_op, batch_source_entry, batch_tgt, box_count)
    merge_density, _, index, op_index = lax.optimization_barrier(
        (fine_density, blocks, index, op_index)
    )
    blocks = lax.all_to_all(blocks, "space", 0, 0, tiled=True)
    partial_sums = merge_upward(
        merge_density, m2m_ops, parent_slot, octant, parent_count, after=m2l_ops
    )
    partial_sums, blocks = lax.optimization_barrier((partial_sums, blocks))
    coarse_level = lax.psum_scatter(partial_sums, "leaf", scatter_dimension=1, tiled=True)
    local_coeffs = translate_lists(fine_density, blocks, m2l_ops, index, op_index)
    return (local_coeffs, coarse_level[:, None, :])


def solution(mesh):
    return jax.shard_map(
        per_device,
        mesh=mesh,
        in_specs=(
            P(None, ("leaf", "space")),
            P(),
            P(),
            P(("leaf", "space")),
            P(("leaf", "space")),
            P(("leaf", "space"), None),
            P(("leaf", "space")),
            P(("leaf", "space"), None),
            P(("leaf", "space"), None),
        ),
        out_specs=(P(None, ("leaf", "space")), P(None, "space", "leaf")),
        check_vma=False,
    )
```
